256 devices in a mesh: pair: 32 (over x, z), aux: 8 (over y, core).
Axes of the slice: x: 4, y: 4, z: 8, core: 2. Of those that a mesh axis runs over, the one named last changes fastest.
Arguments:
- three_centre: bfloat16 [32, 128, 1024, 128], P('pair', None, 'aux'), may hold values from -6 to 6
- green_occ: bfloat16 [160, 128, 128], P('pair'), may hold values from -0.5 to 0.5
- green_virt: bfloat16 [160, 128, 128], P('pair'), may hold values from -0.5 to 0.5
- tile_home: int32 [160], replicated, may hold values from 0 to 159, as said below
- term_source: int32 [32, 7], P('pair'), may hold values from 0 to 2
- term_occ: int32 [32, 7], P('pair'), may hold values from 0 to 159, as said below
- term_virt: int32 [32, 7], P('pair'), may hold values from 0 to 159, as said below
- term_count: int32 [32], P('pair'), may hold values from 2 to 7, as said below
Outputs:
- polarizability: float32 [1024, 1024], P('aux', 'pair')
The draws below stay inside these ranges and needn't reach their ends.
Inputs may be any that keep to these rules, and one draw needn't show every extreme that they name: A permutation: tile id t is stored at row tile_home[t] of green_occ and of green_virt. `term_occ`: counting the occupied and virtual ids of all terms of the 1 block of one pair index together, at most 2 are stored on any one owner (row tile_home[id] lies in owner tile_home[id] // 5); one owner receives exactly 2 from every pair index. Ids in slots at or beyond term_count are valid but unused. `term_virt`: counted together with term_occ as stated there. `term_count`: slots at or beyond this count contribute nothing.
All inputs are finite; a program needn't handle non-finite values.
Results may differ from the reference program's by a relative error of at most 0.0041.
Values may be sent and summed in bfloat16 or wider, within the bound.
A program may use at most 128 MiB of HBM per device.

```python
import math
import jax
import jax.numpy as jnp
from jax import lax

BS = 128
PB_DEV = 1
JMAX = 7
TILE_DEV = 5
NPB = 32
NT = 160
AUX = 1024
CAP = 2
N_PAIR = 32


def tile_plan(key):
    keys = jax.random.split(key, 5)
    home_order = jax.random.permutation(keys[0], NT).astype(jnp.int32)
    request_total = 2 * PB_DEV * JMAX
    busy_owner = jax.random.randint(keys[1], (), 0, N_PAIR).astype(jnp.int32)
    shuffles = jax.vmap(lambda one: jax.random.permutation(one, N_PAIR - 1))(jax.random.split(keys[2], N_PAIR)).astype(jnp.int32)
    others = shuffles + (shuffles >= busy_owner).astype(jnp.int32)
    request_ids = jnp.arange(request_total, dtype=jnp.int32)
    cyclic = (request_ids - CAP) % (N_PAIR - 1)
    owner_list = jnp.where(request_ids[None, :] < CAP, busy_owner, others[:, cyclic])
    reorder = jax.vmap(lambda one: jax.random.permutation(one, request_total))(jax.random.split(keys[3], N_PAIR)).astype(jnp.int32)
    owner_slots = jnp.take_along_axis(owner_list, reorder, axis=1)
    chosen = jax.random.randint(keys[4], (N_PAIR, request_total), 0, TILE_DEV).astype(jnp.int32)
    storage = owner_slots * TILE_DEV + chosen
    inverse = jnp.zeros((NT,), jnp.int32).at[home_order].set(jnp.arange(NT, dtype=jnp.int32))
    logical = inverse[storage].reshape(N_PAIR, 2, PB_DEV, JMAX)
    occ_ids = logical[:, 0].reshape(NPB, JMAX)
    virt_ids = logical[:, 1].reshape(NPB, JMAX)
    return (home_order, occ_ids, virt_ids)


def draw_tile_home(key, part):
    home_order, occ_ids, virt_ids = tile_plan(key)
    return home_order


def draw_term_occ(key, part):
    home_order, occ_ids, virt_ids = tile_plan(key)
    return occ_ids


def draw_term_virt(key, part):
    home_order, occ_ids, virt_ids = tile_plan(key)
    return virt_ids


def draw_term_count(key, part):
    key = jax.random.fold_in(key, 7)
    keys = jax.random.split(key, 3)
    counts = jax.random.randint(keys[0], (NPB,), 2, JMAX + 1).astype(jnp.int32)
    top_place = jax.random.randint(keys[1], (), 0, NPB).astype(jnp.int32)
    low_place = jax.random.randint(keys[2], (), 0, NPB - 1).astype(jnp.int32)
    low_place = low_place + (low_place >= top_place).astype(jnp.int32)
    positions = jnp.arange(NPB, dtype=jnp.int32)
    counts = jnp.where(positions == top_place, JMAX, counts)
    return jnp.where(positions == low_place, 2, counts).astype(jnp.int32)


def with_ends(entries, rng, smallest, largest):
    longest = entries.shape.index(max(entries.shape))
    spots = []
    for shift in (0, 1):
        where = [jax.random.randint(jax.random.fold_in(rng, axis), (), 0, length) for axis, length in enumerate(entries.shape)]
        where[longest] = (where[longest] + shift) % entries.shape[longest]
        spots.append(tuple(where))
    return entries.at[spots[0]].set(smallest).at[spots[1]].set(largest)


def block_scale(key, extent, pieces, low, high):
    level, own = 1.0, jax.random.fold_in(key, 6)
    for axis_at, parts in pieces:
        heights = jnp.exp(jax.random.uniform(jax.random.fold_in(own, axis_at), (parts,), jnp.float32, low / len(pieces), high / len(pieces)))
        level = level * jnp.repeat(heights, extent[axis_at] // parts).reshape([-1 if axis == axis_at else 1 for axis in range(len(extent))])
    return level


def gaussian(rng, dims, spread, reach, pieces=(), held_as=jnp.bfloat16):
    values = jax.random.normal(rng, dims, jnp.float32) * spread
    if len(pieces) > 0:
        values = block_scale(rng, dims, pieces, -0.22, 0.18) * values
    return jnp.clip(values, min=-reach, max=reach).astype(held_as)


def setup_inputs(seed: int = 0) -> dict:
    splits = jax.random.split(jax.random.key(seed), 9)
    three_centre = gaussian(splits[0], (NPB, BS, AUX, BS), 1.0, 6.0, ((0, 32), (2, 8)))
    green_occ = gaussian(splits[1], (NT, BS, BS), BS ** -0.5, 0.5, ((0, 32),))
    green_virt = gaussian(splits[2], (NT, BS, BS), BS ** -0.5, 0.5, ((0, 32),))
    tile_home = draw_tile_home(jax.random.fold_in(splits[8], 71), 0)
    term_source = with_ends(jax.random.randint(splits[4], (NPB, JMAX), 0, 3), jax.random.fold_in(splits[4], 1), 0, 2).astype(jnp.int32)
    term_occ = draw_term_occ(jax.random.fold_in(splits[8], 71), 0)
    term_virt = draw_term_virt(jax.random.fold_in(splits[8], 71), 0)
    term_count = draw_term_count(jax.random.fold_in(splits[8], 71), 0)
    return dict(three_centre=three_centre, green_occ=green_occ, green_virt=green_virt, tile_home=tile_home, term_source=term_source, term_occ=term_occ, term_virt=term_virt, term_count=term_count)


def reference(three_centre, green_occ, green_virt, tile_home, term_source, term_occ, term_virt, term_count):
    block_total = three_centre.shape[0]
    slot_total = term_occ.shape[1]
    occ_tiles = green_occ[tile_home[term_occ]]
    virt_tiles = green_virt[tile_home[term_virt]]
    live_mask = (jnp.arange(slot_total, dtype=jnp.int32)[None, :] < term_count[:, None]).astype(jnp.float32)
    prefactor = -1.0 / (BS * math.sqrt(NPB * JMAX))

    def per_block(running, block_index):

        def add_term(slot_index, accumulated):
            source_index = (block_index + term_source[block_index, slot_index] - 1) % block_total
            source_block = lax.dynamic_index_in_dim(three_centre, source_index.astype(jnp.int32), 0, keepdims=False)
            occ_tile = occ_tiles[block_index, slot_index].astype(jnp.float32)
            half_product = jnp.einsum('lm,lps->mps', occ_tile, source_block.astype(jnp.float32)).astype(jnp.bfloat16)
            weight = virt_tiles[block_index, slot_index].astype(jnp.float32) * live_mask[block_index, slot_index]
            return accumulated + jnp.einsum('mps,sn->mpn', half_product.astype(jnp.float32), weight)
        start = jnp.zeros((BS, AUX, BS), jnp.float32)
        produced = lax.fori_loop(0, slot_total, add_term, start).astype(jnp.bfloat16)
        own_block = lax.dynamic_index_in_dim(three_centre, block_index, 0, keepdims=False)
        term = jnp.einsum('mpn,mqn->pq', produced.astype(jnp.float32), own_block.astype(jnp.float32))
        return (running + term, None)
    summed, unused = lax.scan(per_block, jnp.zeros((AUX, AUX), jnp.float32), jnp.arange(block_total, dtype=jnp.int32))
    return summed * prefactor
```

```python
import functools
import math

import jax
import jax.numpy as jnp
from jax import lax
from jax.experimental import pallas as pl
from jax.experimental.pallas import tpu as pltpu
from jax.sharding import PartitionSpec as P

MESH = pl.DeviceIdType.MESH
BF = jnp.bfloat16
F32 = jnp.float32

BS = 128
NX, NZ, NY = 4, 8, 4
NPAIR = NX * NZ
NAUX = 2 * NY
SLOTS = 7
TILES = 5
PC = 16
CH = BS // PC
DEPTH = 3
GROUP = 2
QP = 4
ROWS = PC * NAUX
QX = 256
QZ = 32


def kernel(
    scale,
    t_hbm, occ_hbm, virt_hbm, home, src, tocc, tvirt, count,
    out,
    tv, xx, gocc, gvirt, sel, tiles, oo, tq, pt, pr, pq, pb, ar, bs, br, rr, cs, cr,
    t_sem, own_sem, bounce, z_ss, z_rs, x_ss, x_rs, s_ss, s_rs, s_own,
    h_ss, h_rs, q_ss, q_rs, q_own, p_ss, p_rs, p_own, a_ss, a_rs, a_own, b_ss, b_rs, b_own,
    c_ss, c_rs, c_own,
):
    k = lax.axis_index("pair")
    a = lax.axis_index("aux")
    x, z, y, c = k // NZ, lax.rem(k, NZ), a // 2, lax.rem(a, 2)
    up, down = lax.rem(k + 1, NPAIR), lax.rem(k + NPAIR - 1, NPAIR)

    def aux_peer(d):
        return lax.rem(a + d, NAUX)

    def z_peer(d):
        return x * NZ + lax.rem(z + d, NZ)

    def x_peer(d):
        return lax.rem(x + d, NX) * NZ + z

    def remote(s, d, ss, rs, dev):
        return pltpu.make_async_remote_copy(
            src_ref=s, dst_ref=d, send_sem=ss, recv_sem=rs, device_id=dev, device_id_type=MESH
        )

    def load(i):
        return pltpu.make_async_copy(
            t_hbm.at[0, :, pl.ds(i * PC, PC), :], tv.at[i], t_sem.at[i]
        )

    myrows = pl.ds(pl.multiple_of(a * 16, 16), 16)

    def tile_z(kind, d):
        hbm, g = ((occ_hbm, gocc), (virt_hbm, gvirt))[kind]
        return remote(
            hbm.at[:, myrows, :], g.at[pl.ds(k * TILES, TILES)],
            z_ss.at[kind, d], z_rs.at[kind, d], (z_peer(d), a),
        )

    def tile_own(kind):
        hbm, g = ((occ_hbm, gocc), (virt_hbm, gvirt))[kind]
        return pltpu.make_async_copy(
            hbm.at[:, myrows, :], g.at[pl.ds(k * TILES, TILES)], own_sem.at[kind]
        )

    def tile_x(kind, d):
        g = (gocc, gvirt)[kind]
        part = pl.ds(x * NZ * TILES, NZ * TILES)
        return remote(
            g.at[part], g.at[part], x_ss.at[kind, d], x_rs.at[kind, d], (x_peer(d), a)
        )

    def tile_s(d):
        return remote(
            sel, tiles.at[:, myrows, :], s_ss.at[d], s_rs.at[d], (k, aux_peer(d))
        )

    def halo(i, side):
        part = pl.ds(i * PC, PC)
        return remote(
            xx.at[1, part], xx.at[2 * side, part],
            h_ss.at[side, i], h_rs.at[side, i], ((down if side else up), a),
        )

    def rows_q(d, part):
        b = aux_peer(d)
        w = BS // QP
        return remote(
            t_hbm.at[0, pl.ds(b * 16, 16), pl.ds(part * w, w), :],
            tq.at[:, pl.ds(pl.multiple_of(a * BS + part * w, 16), w), :],
            q_ss.at[d, part], q_rs.at[d, part], (k, b),
        )

    def rows_own():
        return pltpu.make_async_copy(
            t_hbm.at[0, pl.ds(a * 16, 16)],
            tq.at[:, pl.ds(pl.multiple_of(a * BS, BS), BS), :], q_own.at[0],
        )

    prow = pl.ds(pl.multiple_of((c * NY + y) * PC, PC), PC)

    def prod_s(i, d):
        b = aux_peer(d)
        return remote(
            pr.at[i, pl.ds(b * 16, 16)], pq.at[i, :, prow, :],
            p_ss.at[i, d], p_rs.at[i, d], (k, b),
        )

    def prod_own(i):
        return pltpu.make_async_copy(
            pr.at[i, pl.ds(a * 16, 16)], pq.at[i, :, prow, :], p_own.at[i]
        )

    def part_a(i, e):
        dx, dc = e // 2, e % 2
        cc = lax.rem(c + dc, 2)
        return remote(
            pb.at[i, lax.rem(x + dx, NX), pl.ds(pl.multiple_of(cc * 64, 64), 64), :],
            ar.at[i, e], a_ss.at[i, e], a_rs.at[i, e], (x_peer(dx), y * 2 + cc),
        )

    def part_a_own(i):
        return pltpu.make_async_copy(
            pb.at[i, x, pl.ds(pl.multiple_of(c * 64, 64), 64), :], ar.at[i, 0], a_own.at[i]
        )

    def part_b(i, d):
        yy = lax.rem(y + d, NY)
        return remote(
            bs.at[i, pl.ds(pl.multiple_of(yy * PC, PC), PC), :], br.at[i, d],
            b_ss.at[i, d], b_rs.at[i, d], (k, yy * 2 + c),
        )

    def part_b_own(i):
        return pltpu.make_async_copy(
            bs.at[i, pl.ds(pl.multiple_of(y * PC, PC), PC), :], br.at[i, 0], b_own.at[i]
        )

    def part_c(d):
        zz = lax.rem(z + d, NZ)
        return remote(
            cs.at[pl.ds(pl.multiple_of(zz * QZ, QZ), QZ), :], cr.at[d],
            c_ss.at[d], c_rs.at[d], (z_peer(d), a),
        )

    def part_c_own():
        return pltpu.make_async_copy(
            cs.at[pl.ds(pl.multiple_of(z * QZ, QZ), QZ), :], cr.at[0], c_own.at[0]
        )

    def turn(i):
        load(i).wait()
        xx[1, pl.ds(i * PC, PC)] = jnp.swapaxes(tv[i], 0, 1)

    def start_load(i, carry):
        load(i).start()
        return carry

    lax.fori_loop(0, CH, start_load, 0)
    for kind in range(2):
        tile_own(kind).start()
    rows_own().start()
    barrier = pltpu.get_barrier_semaphore()
    partners = [(up, a), (down, a)]
    partners += [(k, aux_peer(d)) for d in range(1, NAUX)]
    partners += [(z_peer(d), a) for d in range(1, NZ)]
    partners += [
        (x_peer(d), y * 2 + lax.rem(c + dc, 2)) for d in range(1, NX) for dc in range(2)
    ]
    for dev in partners:
        pl.semaphore_signal(barrier, inc=1, device_id=dev, device_id_type=MESH)
    turn(0)
    pl.semaphore_wait(barrier, len(partners))

    def send_halo(i):
        for side in range(2):
            halo(i, side).start()

    def send_rows(part):
        for d in range(1, NAUX):
            rows_q(d, part).start()

    for kind in range(2):
        for d in range(1, NZ):
            tile_z(kind, d).start()
    send_halo(0)
    send_rows(0)

    def first(i, carry):
        turn(i)
        send_halo(i)
        return carry

    lax.fori_loop(1, DEPTH, first, 0)

    def rest(i, carry):
        turn(i)
        return carry

    lax.fori_loop(DEPTH, CH, rest, 0)
    for kind in range(2):
        tile_own(kind).wait()
        for d in range(1, NZ):
            tile_z(kind, d).wait_recv()
    for kind in range(2):
        for d in range(1, NX):
            tile_x(kind, d).start()
    send_rows(1)
    for kind in range(2):
        for d in range(1, NX):
            tile_x(kind, d).wait_recv()
    for j in range(SLOTS):
        sel[j] = gocc[home[tocc[0, j]]]
        sel[SLOTS + j] = gvirt[home[tvirt[0, j]]]
    for d in range(1, NAUX):
        tile_s(d).start()
    keep = pltpu.make_async_copy(sel, tiles.at[:, myrows, :], s_own.at[0])
    keep.start()
    keep.wait()
    for d in range(1, NAUX):
        tile_s(d).wait_recv()

    live = count[0]
    for j in range(SLOTS):
        turned = tiles[j].astype(F32).T
        for s in range(3):
            weight = jnp.where(jnp.logical_and(src[0, j] == s, j < live), 1.0, 0.0)
            oo[pl.ds(j * BS, BS), pl.ds(s * BS, BS)] = (turned * weight).astype(BF)

    def products(i):
        for side in range(2):
            halo(i, side).wait_recv()

        @pl.when(i + DEPTH < CH)
        def _():
            send_halo(i + DEPTH)

        @pl.when(i + 2 < QP)
        def _():
            send_rows(i + 2)

        def group(g, carry):
            p0 = i * PC + g * GROUP
            stacked = jnp.concatenate(
                [
                    jnp.concatenate([xx[s, p0 + u] for u in range(GROUP)], axis=1)
                    for s in range(3)
                ],
                axis=0,
            )
            half = jnp.dot(oo[...], stacked, preferred_element_type=F32).astype(BF)
            side = jnp.concatenate(
                [
                    jnp.concatenate(
                        [
                            half[j * BS:(j + 1) * BS, u * BS:(u + 1) * BS]
                            for j in range(SLOTS)
                        ],
                        axis=1,
                    )
                    for u in range(GROUP)
                ],
                axis=0,
            )
            virt = tiles[pl.ds(SLOTS, SLOTS)].reshape(SLOTS * BS, BS)
            prod = jnp.dot(side, virt, preferred_element_type=F32).astype(BF)
            pt[pl.ds(g * GROUP, GROUP)] = prod.reshape(GROUP, BS, BS)
            return carry

        lax.fori_loop(0, PC // GROUP, group, 0)
        pr[i] = jnp.swapaxes(pt[...], 0, 1)
        prod_own(i).start()
        for d in range(1, NAUX):
            prod_s(i, d).start()

    def contract(i):
        prod_own(i).wait()
        for d in range(1, NAUX):
            prod_s(i, d).wait_recv()

        def block(n, carry):
            left = jnp.concatenate([pq[i, m] for m in range(16)], axis=1)
            qs = pl.ds(pl.multiple_of(n * QX, QX), QX)
            right = jnp.concatenate([tq[m, qs, :] for m in range(16)], axis=1)
            pb[i, n] = lax.dot_general(
                left, right, (((1,), (1,)), ((), ())), preferred_element_type=F32
            ).astype(BF)
            return carry

        lax.fori_loop(0, NX, block, 0)
        part_a_own(i).start()
        for e in range(1, 2 * NX):
            part_a(i, e).start()

    def add_a(i):
        part_a_own(i).wait()
        for e in range(1, 2 * NX):
            part_a(i, e).wait_recv()
        total = ar[i, 0].astype(F32)
        for e in range(1, 2 * NX):
            total = total + ar[i, e].astype(F32)
        bs[i] = total
        part_b_own(i).start()
        for d in range(1, NY):
            part_b(i, d).start()

    def add_b(i):
        part_b_own(i).wait()
        for d in range(1, NY):
            part_b(i, d).wait_recv()
        total = br[i, 0]
        for d in range(1, NY):
            total = total + br[i, d]
        rr[pl.ds(pl.multiple_of(i * PC, PC), PC), :] = total

    def step(i, carry):
        @pl.when(i < CH)
        def _():
            products(i)

        @pl.when(i == 1)
        def _():
            rows_own().wait()
            for part in range(QP):
                for d in range(1, NAUX):
                    rows_q(d, part).wait_recv()

        @pl.when(jnp.logical_and(i >= 1, i <= CH))
        def _():
            contract(i - 1)

        @pl.when(jnp.logical_and(i >= 2, i <= CH + 1))
        def _():
            add_a(i - 2)

        @pl.when(i >= 3)
        def _():
            add_b(i - 3)

        return carry

    lax.fori_loop(0, CH + 3, step, 0)

    cs[...] = rr[...].T
    part_c_own().start()
    for d in range(1, NZ):
        part_c(d).start()
    part_c_own().wait()
    for d in range(1, NZ):
        part_c(d).wait_recv()
    total = cr[0]
    for d in range(1, NZ):
        total = total + cr[d]
    out[...] = total.T * scale

    for kind in range(2):
        for d in range(1, NZ):
            tile_z(kind, d).wait_send()
        for d in range(1, NX):
            tile_x(kind, d).wait_send()
    for d in range(1, NAUX):
        tile_s(d).wait_send()
        for part in range(QP):
            rows_q(d, part).wait_send()

    def drain(i, carry):
        for side in range(2):
            halo(i, side).wait_send()
        for d in range(1, NAUX):
            prod_s(i, d).wait_send()
        for e in range(1, 2 * NX):
            part_a(i, e).wait_send()
        for d in range(1, NY):
            part_b(i, d).wait_send()
        return carry

    lax.fori_loop(0, CH, drain, 0)
    for d in range(1, NZ):
        part_c(d).wait_send()


def body(three_centre, green_occ, green_virt, tile_home, term_source, term_occ, term_virt, term_count):
    vm = pltpu.VMEM
    dma = pltpu.SemaphoreType.DMA
    scale = -1.0 / (BS * math.sqrt(NPAIR * SLOTS))
    hbm = pl.BlockSpec(memory_space=pl.ANY)
    smem = pl.BlockSpec(memory_space=pltpu.SMEM)
    return pl.pallas_call(
        functools.partial(kernel, scale),
        out_shape=jax.ShapeDtypeStruct((BS, QZ), F32),
        in_specs=[hbm] * 3 + [smem] * 5,
        out_specs=pl.BlockSpec(memory_space=pltpu.VMEM),
        scratch_shapes=[
            vm((CH, BS, PC, BS), BF),
            vm((3, BS, BS, BS), BF),
            vm((NPAIR * TILES, 16, BS), BF),
            vm((NPAIR * TILES, 16, BS), BF),
            vm((2 * SLOTS, 16, BS), BF),
            vm((2 * SLOTS, BS, BS), BF),
            vm((SLOTS * BS, 3 * BS), BF),
            vm((16, NAUX * BS, BS), BF),
            vm((PC, BS, BS), BF),
            vm((CH, BS, PC, BS), BF),
            vm((CH, 16, ROWS, BS), BF),
            vm((CH, NX, ROWS, QX), BF),
            vm((CH, 2 * NX, 64, QX), BF),
            vm((CH, 64, QX), F32),
            vm((CH, NY, PC, QX), F32),
            vm((BS, QX), F32),
            vm((QX, BS), F32),
            vm((NZ, QZ, BS), F32),
            dma((CH,)), dma((2,)), dma((1,)),
            dma((2, NZ)), dma((2, NZ)), dma((2, NX)), dma((2, NX)),
            dma((NAUX,)), dma((NAUX,)), dma((1,)),
            dma((2, CH)), dma((2, CH)),
            dma((NAUX, QP)), dma((NAUX, QP)), dma((1,)),
            dma((CH, NAUX)), dma((CH, NAUX)), dma((CH,)),
            dma((CH, 2 * NX)), dma((CH, 2 * NX)), dma((CH,)),
            dma((CH, NY)), dma((CH, NY)), dma((CH,)),
            dma((NZ,)), dma((NZ,)), dma((1,)),
        ],
        compiler_params=pltpu.CompilerParams(
            collective_id=0, has_side_effects=True, vmem_limit_bytes=60 * 2**20
        ),
    )(three_centre, green_occ, green_virt, tile_home, term_source, term_occ, term_virt, term_count)


def solution(mesh):
    in_specs = (
        P("pair", None, "aux", None),
        P("pair", None, None),
        P("pair", None, None),
        P(),
        P("pair", None),
        P("pair", None),
        P("pair", None),
        P("pair"),
    )
    return jax.shard_map(
        body, mesh=mesh, in_specs=in_specs, out_specs=P("aux", "pair"), check_vma=False
    )
```

```python
import functools
import math

import jax
import jax.numpy as jnp
from jax import lax
from jax.experimental import pallas as pl
from jax.experimental.pallas import tpu as pltpu
from jax.sharding import PartitionSpec as P

MESH = pl.DeviceIdType.MESH
BF = jnp.bfloat16
F32 = jnp.float32

BS = 128
NX, NZ, NY = 4, 8, 4
NPAIR = NX * NZ
NAUX = 2 * NY
SLOTS = 7
TILES = 5
PC = 16
CH = BS // PC
DEPTH = 3
EARLY = 5
LAG = 3
GROUP = 2
QP = 4
ROWS = PC * NAUX
QX = 256
QZ = 32


def kernel(
    scale,
    t_hbm, occ_hbm, virt_hbm, home, src, tocc, tvirt, count,
    out,
    tv, xx, gocc, gvirt, ask, asked, given, got, sel, tiles, oo, tq, pt, pr, pq, pb, ar, bs, br, rr, cs, cr,
    bounce, t_sem, own_sem, e_ss, e_rs, f_ss, z_ss, z_rs, w_ss, w_rs, x_ss, x_rs, s_ss, s_rs, s_own,
    h_ss, h_rs, q_ss, q_rs, q_own, p_ss, p_rs, p_own, a_ss, a_rs, a_own, b_ss, b_rs, b_own,
    c_ss, c_rs, c_own,
):
    k = lax.axis_index("pair")
    a = lax.axis_index("aux")
    x, z, y, c = k // NZ, lax.rem(k, NZ), a // 2, lax.rem(a, 2)
    up, down = lax.rem(k + 1, NPAIR), lax.rem(k + NPAIR - 1, NPAIR)

    def aux_peer(d):
        return lax.rem(a + d, NAUX)

    def z_peer(d):
        return x * NZ + lax.rem(z + d, NZ)

    def x_peer(d):
        return lax.rem(x + d, NX) * NZ + z

    def remote(s, d, ss, rs, dev):
        return pltpu.make_async_remote_copy(
            src_ref=s, dst_ref=d, send_sem=ss, recv_sem=rs, device_id=dev, device_id_type=MESH
        )

    def load(i):
        return pltpu.make_async_copy(
            t_hbm.at[0, :, pl.ds(i * PC, PC), :], tv.at[i], t_sem.at[i]
        )

    myrows = pl.ds(pl.multiple_of(a * 16, 16), 16)

    def tile_z(kind, d):
        hbm, g = ((occ_hbm, gocc), (virt_hbm, gvirt))[kind]
        return remote(
            hbm.at[:, myrows, :], g.at[pl.ds(z * TILES, TILES)],
            z_ss.at[kind, d], z_rs.at[kind, d], (z_peer(d), a),
        )

    def tile_own(kind):
        hbm, g = ((occ_hbm, gocc), (virt_hbm, gvirt))[kind]
        return pltpu.make_async_copy(
            hbm.at[:, myrows, :], g.at[pl.ds(z * TILES, TILES)], own_sem.at[kind]
        )

    def wish(d):
        return remote(ask.at[0], ask.at[d], w_ss.at[d], w_rs.at[d], (x_peer(d), a))

    def tile_x(d):
        return remote(
            given.at[d], got.at[d], x_ss.at[d], x_rs.at[d], (x_peer(NX - d), a)
        )

    def tile_s(d):
        return remote(
            sel, tiles.at[:, myrows, :], s_ss.at[d], s_rs.at[d], (k, aux_peer(d))
        )

    def halo(i, side):
        part = pl.ds(i * PC, PC)
        return remote(
            xx.at[1, part], xx.at[2 * side, part],
            h_ss.at[side, i], h_rs.at[side, i], ((down if side else up), a),
        )

    edge = jnp.logical_or(z == 0, z == NZ - 1)
    at_top = z // (NZ - 1)
    edge_side = 1 - at_top
    beyond = lax.rem(x + NX + 2 * at_top - 1, NX) * NZ + z

    def halo_half(i, side):
        part = pl.ds(i * PC, PC // 2)
        return remote(
            xx.at[1, part], xx.at[2 * side, part],
            h_ss.at[side, i], h_rs.at[side, i], ((down if side else up), a),
        )

    def halo_away(i):
        return remote(
            xx.at[1, pl.ds(i * PC + PC // 2, PC // 2)], bounce.at[i],
            e_ss.at[i], e_rs.at[i], (beyond, a),
        )

    def halo_on(i):
        return remote(
            bounce.at[i], xx.at[2 * edge_side, pl.ds(i * PC + PC // 2, PC // 2)],
            f_ss.at[i], h_rs.at[edge_side, i], (x * NZ + NZ - 1 - z, a),
        )

    def send_on(i):
        @pl.when(edge)
        def _():
            halo_away(i).wait_recv()
            halo_on(i).start()

    def rows_q(d, part):
        b = aux_peer(d)
        w = BS // QP
        return remote(
            t_hbm.at[0, pl.ds(b * 16, 16), pl.ds(part * w, w), :],
            tq.at[:, pl.ds(pl.multiple_of(a * BS + part * w, 16), w), :],
            q_ss.at[d, part], q_rs.at[d, part], (k, b),
        )

    def rows_own():
        return pltpu.make_async_copy(
            t_hbm.at[0, pl.ds(a * 16, 16)],
            tq.at[:, pl.ds(pl.multiple_of(a * BS, BS), BS), :], q_own.at[0],
        )

    prow = pl.ds(pl.multiple_of((c * NY + y) * PC, PC), PC)

    def prod_s(i, d):
        b = aux_peer(d)
        return remote(
            pr.at[i, pl.ds(b * 16, 16)], pq.at[i, :, prow, :],
            p_ss.at[i, d], p_rs.at[i, d], (k, b),
        )

    def prod_own(i):
        return pltpu.make_async_copy(
            pr.at[i, pl.ds(a * 16, 16)], pq.at[i, :, prow, :], p_own.at[i]
        )

    def part_a(i, e):
        dx, dc = e // 2, e % 2
        cc = lax.rem(c + dc, 2)
        return remote(
            pb.at[i, lax.rem(x + dx, NX), pl.ds(pl.multiple_of(cc * 64, 64), 64), :],
            ar.at[i, e], a_ss.at[i, e], a_rs.at[i, e], (x_peer(dx), y * 2 + cc),
        )

    def part_a_own(i):
        return pltpu.make_async_copy(
            pb.at[i, x, pl.ds(pl.multiple_of(c * 64, 64), 64), :], ar.at[i, 0], a_own.at[i]
        )

    def part_b(i, d):
        yy = lax.rem(y + d, NY)
        return remote(
            bs.at[i, pl.ds(pl.multiple_of(yy * PC, PC), PC), :], br.at[i, d],
            b_ss.at[i, d], b_rs.at[i, d], (k, yy * 2 + c),
        )

    def part_b_own(i):
        return pltpu.make_async_copy(
            bs.at[i, pl.ds(pl.multiple_of(y * PC, PC), PC), :], br.at[i, 0], b_own.at[i]
        )

    def part_c(d):
        zz = lax.rem(z + d, NZ)
        return remote(
            cs.at[pl.ds(pl.multiple_of(zz * QZ, QZ), QZ), :], cr.at[d],
            c_ss.at[d], c_rs.at[d], (z_peer(d), a),
        )

    def part_c_own():
        return pltpu.make_async_copy(
            cs.at[pl.ds(pl.multiple_of(z * QZ, QZ), QZ), :], cr.at[0], c_own.at[0]
        )

    def turn(i):
        load(i).wait()
        xx[1, pl.ds(i * PC, PC)] = jnp.swapaxes(tv[i], 0, 1)

    def start_load(i, carry):
        load(i).start()
        return carry

    lax.fori_loop(0, CH, start_load, 0)
    for kind in range(2):
        tile_own(kind).start()
    rows_own().start()
    barrier = pltpu.get_barrier_semaphore()
    partners = [(up, a), (down, a)]
    partners += [(k, aux_peer(d)) for d in range(1, NAUX)]
    partners += [(z_peer(d), a) for d in range(1, NZ)]
    partners += [
        (x_peer(d), y * 2 + lax.rem(c + dc, 2)) for d in range(1, NX) for dc in range(2)
    ]
    for dev in partners:
        pl.semaphore_signal(barrier, inc=1, device_id=dev, device_id_type=MESH)
    lane = lax.broadcasted_iota(jnp.int32, (8, BS), 1)
    wanted = jnp.zeros((8, BS), jnp.int32)
    for j in range(SLOTS):
        wanted = jnp.where(lane == j, home[tocc[0, j]], wanted)
        wanted = jnp.where(lane == SLOTS + j, home[tvirt[0, j]], wanted)
    ask[0] = wanted
    turn(0)
    pl.semaphore_wait(barrier, len(partners))

    def send_halo(i):
        for side, last in ((0, NZ - 1), (1, 0)):

            @pl.when(z == last)
            def _():
                halo_half(i, side).start()
                halo_away(i).start()

            @pl.when(z != last)
            def _():
                halo(i, side).start()

    def send_rows(part):
        for d in range(1, NAUX):
            rows_q(d, part).start()

    for d in range(1, NX):
        wish(d).start()
    for kind in range(2):
        for d in range(1, NZ):
            tile_z(kind, d).start()
    send_rows(0)
    send_halo(0)

    def rest(i, carry):
        turn(i)
        return carry

    lax.fori_loop(1, CH, rest, 0)
    for d in range(1, NX):
        wish(d).wait_recv()
    read = pltpu.make_async_copy(ask, asked, s_own.at[1])
    read.start()
    read.wait()
    for kind in range(2):
        tile_own(kind).wait()
        for d in range(1, NZ):
            tile_z(kind, d).wait_recv()
    for d in range(NX):
        for j in range(2 * SLOTS):
            g = gocc if j < SLOTS else gvirt
            row = jnp.clip(asked[d, 0, j] - x * (NZ * TILES), 0, NZ * TILES - 1)
            if d == 0:
                got[0, j] = g[row]
            else:
                given[d, j] = g[row]
        if d > 0:
            tile_x(d).start()

    def first(i, carry):
        send_halo(i)
        return carry

    lax.fori_loop(1, DEPTH, first, 0)
    send_on(0)
    for d in range(1, NX):
        tile_x(d).wait_recv()
    for j in range(2 * SLOTS):
        owner = asked[0, 0, j] // (NZ * TILES)
        sel[j] = got[lax.rem(owner + NX - x, NX), j]
    for d in range(1, NAUX):
        tile_s(d).start()
    keep = pltpu.make_async_copy(sel, tiles.at[:, myrows, :], s_own.at[0])
    keep.start()
    keep.wait()
    send_rows(1)
    for i in range(1, DEPTH - 1):
        send_on(i)
    for i in range(DEPTH, EARLY):
        send_halo(i)
    for d in range(1, NAUX):
        tile_s(d).wait_recv()

    for part in range(2, QP):
        send_rows(part)
    live = count[0]
    for j in range(SLOTS):
        turned = tiles[j].astype(F32).T
        for s in range(3):
            weight = jnp.where(jnp.logical_and(src[0, j] == s, j < live), 1.0, 0.0)
            oo[pl.ds(j * BS, BS), pl.ds(s * BS, BS)] = (turned * weight).astype(BF)

    def products(i):
        @pl.when(i + DEPTH - 1 < CH)
        def _():
            send_on(i + DEPTH - 1)

        for side in range(2):
            halo(i, side).wait_recv()

        @pl.when(jnp.logical_and(i + DEPTH >= EARLY, i + DEPTH < CH))
        def _():
            send_halo(i + DEPTH)

        def group(g, carry):
            p0 = i * PC + g * GROUP
            stacked = jnp.concatenate(
                [
                    jnp.concatenate([xx[s, p0 + u] for u in range(GROUP)], axis=1)
                    for s in range(3)
                ],
                axis=0,
            )
            half = jnp.dot(oo[...], stacked, preferred_element_type=F32).astype(BF)
            side = jnp.concatenate(
                [
                    jnp.concatenate(
                        [
                            half[j * BS:(j + 1) * BS, u * BS:(u + 1) * BS]
                            for j in range(SLOTS)
                        ],
                        axis=1,
                    )
                    for u in range(GROUP)
                ],
                axis=0,
            )
            virt = tiles[pl.ds(SLOTS, SLOTS)].reshape(SLOTS * BS, BS)
            prod = jnp.dot(side, virt, preferred_element_type=F32).astype(BF)
            pt[pl.ds(g * GROUP, GROUP)] = prod.reshape(GROUP, BS, BS)
            return carry

        lax.fori_loop(0, PC // GROUP, group, 0)
        pr[i] = jnp.swapaxes(pt[...], 0, 1)
        prod_own(i).start()
        for d in range(1, NAUX):
            prod_s(i, d).start()

    def contract(i):
        prod_own(i).wait()
        for d in range(1, NAUX):
            prod_s(i, d).wait_recv()

        def block(n, carry):
            left = jnp.concatenate([pq[i, m] for m in range(16)], axis=1)
            qs = pl.ds(pl.multiple_of(n * QX, QX), QX)
            right = jnp.concatenate([tq[m, qs, :] for m in range(16)], axis=1)
            pb[i, n] = lax.dot_general(
                left, right, (((1,), (1,)), ((), ())), preferred_element_type=F32
            ).astype(BF)
            return carry

        lax.fori_loop(0, NX, block, 0)
        part_a_own(i).start()
        for e in range(1, 2 * NX):
            part_a(i, e).start()

    def add_a(i):
        part_a_own(i).wait()
        for e in range(1, 2 * NX):
            part_a(i, e).wait_recv()
        total = ar[i, 0].astype(F32)
        for e in range(1, 2 * NX):
            total = total + ar[i, e].astype(F32)
        bs[i] = total
        part_b_own(i).start()
        for d in range(1, NY):
            part_b(i, d).start()

    def add_b(i):
        part_b_own(i).wait()
        for d in range(1, NY):
            part_b(i, d).wait_recv()
        total = br[i, 0]
        for d in range(1, NY):
            total = total + br[i, d]
        rr[pl.ds(pl.multiple_of(i * PC, PC), PC), :] = total

    def step(i, carry):
        @pl.when(i < CH)
        def _():
            products(i)

        @pl.when(i == LAG)
        def _():
            rows_own().wait()
            for part in range(QP):
                for d in range(1, NAUX):
                    rows_q(d, part).wait_recv()

        @pl.when(jnp.logical_and(i >= LAG, i < CH + LAG))
        def _():
            contract(i - LAG)

        @pl.when(jnp.logical_and(i >= LAG + 1, i < CH + LAG + 1))
        def _():
            add_a(i - LAG - 1)

        @pl.when(i >= LAG + 2)
        def _():
            add_b(i - LAG - 2)

        return carry

    lax.fori_loop(0, CH + LAG + 2, step, 0)

    cs[...] = rr[...].T
    part_c_own().start()
    for d in range(1, NZ):
        part_c(d).start()
    part_c_own().wait()
    for d in range(1, NZ):
        part_c(d).wait_recv()
    total = cr[0]
    for d in range(1, NZ):
        total = total + cr[d]
    out[...] = total.T * scale

    for kind in range(2):
        for d in range(1, NZ):
            tile_z(kind, d).wait_send()
    for d in range(1, NX):
        wish(d).wait_send()
        tile_x(d).wait_send()
    for d in range(1, NAUX):
        tile_s(d).wait_send()
        for part in range(QP):
            rows_q(d, part).wait_send()

    def drain(i, carry):
        for side, last in ((0, NZ - 1), (1, 0)):

            @pl.when(z == last)
            def _():
                halo_half(i, side).wait_send()
                halo_away(i).wait_send()
                halo_on(i).wait_send()

            @pl.when(z != last)
            def _():
                halo(i, side).wait_send()

        for d in range(1, NAUX):
            prod_s(i, d).wait_send()
        for e in range(1, 2 * NX):
            part_a(i, e).wait_send()
        for d in range(1, NY):
            part_b(i, d).wait_send()
        return carry

    lax.fori_loop(0, CH, drain, 0)
    for d in range(1, NZ):
        part_c(d).wait_send()


def body(three_centre, green_occ, green_virt, tile_home, term_source, term_occ, term_virt, term_count):
    vm = pltpu.VMEM
    dma = pltpu.SemaphoreType.DMA
    scale = -1.0 / (BS * math.sqrt(NPAIR * SLOTS))
    hbm = pl.BlockSpec(memory_space=pl.ANY)
    smem = pl.BlockSpec(memory_space=pltpu.SMEM)
    return pl.pallas_call(
        functools.partial(kernel, scale),
        out_shape=jax.ShapeDtypeStruct((BS, QZ), F32),
        in_specs=[hbm] * 3 + [smem] * 5,
        out_specs=pl.BlockSpec(memory_space=pltpu.VMEM),
        scratch_shapes=[
            vm((CH, BS, PC, BS), BF),
            vm((3, BS, BS, BS), BF),
            vm((NZ * TILES, 16, BS), BF),
            vm((NZ * TILES, 16, BS), BF),
            vm((NX, 8, BS), jnp.int32),
            pltpu.SMEM((NX, 8, BS), jnp.int32),
            vm((NX, 2 * SLOTS, 16, BS), BF),
            vm((NX, 2 * SLOTS, 16, BS), BF),
            vm((2 * SLOTS, 16, BS), BF),
            vm((2 * SLOTS, BS, BS), BF),
            vm((SLOTS * BS, 3 * BS), BF),
            vm((16, NAUX * BS, BS), BF),
            vm((PC, BS, BS), BF),
            vm((CH, BS, PC, BS), BF),
            vm((CH, 16, ROWS, BS), BF),
            vm((CH, NX, ROWS, QX), BF),
            vm((CH, 2 * NX, 64, QX), BF),
            vm((CH, 64, QX), F32),
            vm((CH, NY, PC, QX), F32),
            vm((BS, QX), F32),
            vm((QX, BS), F32),
            vm((NZ, QZ, BS), F32),
            vm((CH, PC // 2, BS, BS), BF),
            dma((CH,)), dma((2,)), dma((CH,)), dma((CH,)), dma((CH,)),
            dma((2, NZ)), dma((2, NZ)), dma((NX,)), dma((NX,)), dma((NX,)), dma((NX,)),
            dma((NAUX,)), dma((NAUX,)), dma((2,)),
            dma((2, CH)), dma((2, CH)),
            dma((NAUX, QP)), dma((NAUX, QP)), dma((1,)),
            dma((CH, NAUX)), dma((CH, NAUX)), dma((CH,)),
            dma((CH, 2 * NX)), dma((CH, 2 * NX)), dma((CH,)),
            dma((CH, NY)), dma((CH, NY)), dma((CH,)),
            dma((NZ,)), dma((NZ,)), dma((1,)),
        ],
        compiler_params=pltpu.CompilerParams(
            collective_id=0, has_side_effects=True, vmem_limit_bytes=60 * 2**20
        ),
    )(three_centre, green_occ, green_virt, tile_home, term_source, term_occ, term_virt, term_count)


def solution(mesh):
    in_specs = (
        P("pair", None, "aux", None),
        P("pair", None, None),
        P("pair", None, None),
        P(),
        P("pair", None),
        P("pair", None),
        P("pair", None),
        P("pair"),
    )
    return jax.shard_map(
        body, mesh=mesh, in_specs=in_specs, out_specs=P("aux", "pair"), check_vma=False
    )
```
